512 devices in a mesh: ctx: 64 (over z, y), tp: 8 (over x, core).
Axes of the slice: x: 4, y: 4, z: 16, core: 2. Of those that a mesh axis runs over, the one named last changes fastest.
Arguments:
- queries: bfloat16 [16384, 8192], P('ctx', 'tp'), may hold values from -6 to 6
- keys_values: bfloat16 [2, 16384, 1024], P(None, 'ctx', 'tp'), may hold values from -6 to 6
- segments: int32 [16384], P('ctx'), may hold values from 0 to 15, never falling along the last dimension, each value on 1 to 4096 neighbouring positions
Outputs:
- attended: bfloat16 [16384, 8192], P('ctx', 'tp')
The draws below stay inside these ranges and needn't reach their ends.
Inputs may be any that keep to these rules, and one draw needn't show every extreme that they name: `segments`: document ids never fall along the tokens; every document holds 1 to 4096 tokens, and one holds exactly 4096.
All inputs are finite; a program needn't handle non-finite values.
Results may differ from the reference program's by a relative error of at most 0.012.
Values may be sent and summed in bfloat16 or wider, within the bound.
No kernel may reach another device: no remote copies, remote signals or barrier semaphores. Data moves between devices by JAX's collectives and lax.ppermute only.
A program may use at most 64 MiB of HBM per device.

```python
import math
import jax
import jax.numpy as jnp
import numpy as np
from jax import lax

HEADS = 64
KV = 8
HD = 128
MAXDOC = 4096
TOKENS = 16384
DOCS = 16


def base_keys(key):
    return jax.random.normal(key, (TOKENS, KV * HD), jnp.float32)


def draw_keys_values(key, part):
    key_rows = base_keys(key)
    key = jax.random.fold_in(key, 3)
    value_rows = jax.random.normal(key, (TOKENS, KV * HD), jnp.float32)
    key_rows = jnp.clip(key_rows, -6.0, 6.0)
    value_rows = jnp.clip(value_rows, -6.0, 6.0)
    return jnp.stack([key_rows, value_rows]).astype(jnp.bfloat16)


def draw_queries(key, part):
    key = jax.random.fold_in(key, 4)
    chosen = jax.random.normal(key, (TOKENS, HEADS * HD), jnp.float32)
    return jnp.clip(chosen, -6.0, 6.0).astype(jnp.bfloat16)


def profile(number_of, total, limit, slope):
    loads = [(1 << 20) // math.isqrt(rank ** slope) + 1 for rank in range(2, number_of + 1)]
    surplus, given = total - limit - (number_of - 1), [1] * (number_of - 1)
    while surplus > 0:
        movable = [i for i in range(number_of - 1) if given[i] < limit]
        whole, left = sum([loads[i] for i in movable]), surplus
        for i in movable:
            extra = min(limit - given[i], max(1, left * loads[i] // whole), surplus)
            given[i] = given[i] + extra
            surplus = surplus - extra
    return np.array([limit] + given)


def ragged(stream_key, number_of, total, bound, slope):
    if number_of == 2:
        one = jax.random.randint(stream_key, (), max(1, total - bound), min(bound, total - 1) + 1)
        return jnp.stack([one, total - one])
    sizes = jnp.asarray(profile(number_of, total, bound, slope), jnp.int32)
    pairs = (number_of - 1) // 2
    source_of, sink = sizes[1:1 + 2 * pairs:2], sizes[2:2 + 2 * pairs:2]
    margin = jnp.minimum(source_of - 1, bound - sink)
    shifted = jax.random.randint(jax.random.fold_in(stream_key, 1), (pairs,), 0, 1 << 20) % (margin + 1)
    sizes = sizes.at[1:1 + 2 * pairs:2].set(source_of - shifted).at[2:2 + 2 * pairs:2].set(sink + shifted)
    return sizes[jax.random.permutation(jax.random.fold_in(stream_key, 2), number_of)]


def setup_inputs(seed: int = 0) -> dict:
    arg_keys = jax.random.split(jax.random.key(seed), 4)
    return {
        "queries": draw_queries(jax.random.fold_in(arg_keys[3], 71), 0),
        "keys_values": draw_keys_values(jax.random.fold_in(arg_keys[3], 71), 0),
        "segments": jnp.searchsorted(jnp.cumsum(ragged(arg_keys[2], DOCS, TOKENS, MAXDOC, 2)), jnp.arange(TOKENS), side="right").astype(jnp.int32),
    }


def head_block(q_head, k_head, v_head, visible):
    scores = jnp.einsum("gbd,wd->gbw", q_head, k_head) * (HD ** -0.5)
    scores = jnp.where(visible[None], scores, -jnp.inf)
    peak = jnp.max(scores, axis=-1, keepdims=True)
    log_total = peak + jnp.log(jnp.sum(jnp.exp(scores - peak), axis=-1, keepdims=True))
    weights = jnp.exp(scores - log_total).astype(jnp.bfloat16)
    weights = lax.optimization_barrier(weights).astype(jnp.float32)
    return jnp.einsum("gbw,wd->gbd", weights, v_head)


def reference(queries, keys_values, segments):
    block = 512
    window = MAXDOC + block
    group_size = HEADS // KV
    front = jnp.zeros((MAXDOC, KV * HD), keys_values.dtype)
    key_pad = jnp.concatenate([front, keys_values[0]], axis=0)
    value_pad = jnp.concatenate([front, keys_values[1]], axis=0)
    doc_pad = jnp.concatenate([jnp.full((MAXDOC,), -1, jnp.int32), segments.astype(jnp.int32)])

    def one_block(index):
        start = (index * block).astype(jnp.int32)
        q_rows = lax.dynamic_slice_in_dim(queries, start, block).astype(jnp.float32)
        q_rows = q_rows.reshape(block, KV, group_size, HD).transpose(1, 2, 0, 3)
        k_rows = lax.dynamic_slice_in_dim(key_pad, start, window).astype(jnp.float32)
        k_rows = k_rows.reshape(window, KV, HD).transpose(1, 0, 2)
        v_rows = lax.dynamic_slice_in_dim(value_pad, start, window).astype(jnp.float32)
        v_rows = v_rows.reshape(window, KV, HD).transpose(1, 0, 2)
        query_docs = lax.dynamic_slice_in_dim(segments.astype(jnp.int32), start, block)
        key_docs = lax.dynamic_slice_in_dim(doc_pad, start, window)
        query_pos = jnp.arange(block, dtype=jnp.int32) + MAXDOC
        key_pos = jnp.arange(window, dtype=jnp.int32)
        visible = (query_docs[:, None] == key_docs[None, :]) & (key_pos[None, :] <= query_pos[:, None])

        def one_head(operands):
            return head_block(operands[0], operands[1], operands[2], visible)

        outputs = lax.map(one_head, (q_rows, k_rows, v_rows))
        return outputs.transpose(2, 0, 1, 3).reshape(block, HEADS * HD).astype(jnp.bfloat16)

    attended = lax.map(one_block, jnp.arange(TOKENS // block, dtype=jnp.int32))
    return attended.reshape(TOKENS, HEADS * HD)
```

```python
import functools
import itertools
import jax
import jax.numpy as jnp
from jax import lax
from jax.experimental import pallas as pl
from jax.experimental.pallas import tpu as pltpu
from jax.sharding import PartitionSpec as P

HD = 128
FAR = 1e30
FACTOR = HD ** (-0.5) * 1.4426950408889634
F32, BF16 = jnp.float32, jnp.bfloat16
NT = (((1,), (1,)), ((), ()))
YS = 4
ROUNDS = ((0, 1), (2, 3))


def pack_kernel(kv_ref, docs_ref, piece_ref, rows_ref):
    tok = kv_ref.shape[1]
    piece_ref[0:tok] = kv_ref[0]
    piece_ref[tok : 2 * tok] = kv_ref[1]
    docs = docs_ref[...].astype(F32)
    n = docs.shape[0]
    piece_ref[2 * tok :] = jnp.concatenate([docs, jnp.zeros((16 - n, HD), F32)], 0).astype(BF16)
    for t in range(n):
        rows_ref[t * HD : (t + 1) * HD] = jnp.broadcast_to(docs[t : t + 1], (HD, HD)).T


def key_docs(piece_ref, lead, tok):
    tail = piece_ref[lead + (slice(2 * tok, 2 * tok + 16),)].astype(F32)
    return jnp.concatenate([tail[t : t + 1] for t in range(tok // HD)], 1)


def own_kernel(q_ref, rows_ref, piece_ref, m_ref, l_ref, acc_ref):
    tok = q_ref.shape[0]
    keys = piece_ref[0:tok]
    values = jnp.concatenate([piece_ref[tok : 2 * tok], jnp.ones((tok, HD), BF16)], 1)
    docs = key_docs(piece_ref, (), tok)
    seen = (rows_ref[:, 0:1] == docs) & (
        lax.broadcasted_iota(jnp.int32, (tok, tok), 1) <= lax.broadcasted_iota(jnp.int32, (tok, tok), 0)
    )
    for h in range(q_ref.shape[1] // HD):
        s = lax.dot_general(q_ref[:, h * HD : (h + 1) * HD], keys, NT, preferred_element_type=F32)
        s = jnp.where(seen, s, -FAR)
        m = jnp.max(s, 1, keepdims=True)
        p = jnp.exp2((s - m) * FACTOR).astype(BF16)
        o = jnp.dot(p, values, preferred_element_type=F32)
        m_ref[h] = jnp.broadcast_to(m, (tok, HD))
        acc_ref[h] = o[:, :HD]
        l_ref[h] = o[:, HD:]


def far_kernel(last, n_refs, *refs):
    q_ref, rows_ref = refs[:2]
    piece_refs = refs[2 : 2 + n_refs]
    m_in, l_in, acc_in = refs[2 + n_refs : 5 + n_refs]
    outs = refs[5 + n_refs : -2]
    s_ref, mx_ref = refs[-2:]
    tok = q_ref.shape[0]
    heads = q_ref.shape[1] // HD
    pieces = [(r, i) for r in piece_refs for i in itertools.product(*[range(s) for s in r.shape[:-2]])]
    first = rows_ref[0:1, 0:1]
    row_off = jnp.where(rows_ref[...] == first, 0.0, FAR)
    bias = [jnp.where(key_docs(r, i, tok) == first, 0.0, -FAR) for r, i in pieces]

    def score(h, slot):
        q = q_ref[:, pl.ds(pl.multiple_of(h * HD, HD), HD)]
        mx = None
        for k, (r, i) in enumerate(pieces):
            s = lax.dot_general(q, r[i + (slice(0, tok),)], NT, preferred_element_type=F32) + bias[k]
            s_ref[slot, :, k * tok : (k + 1) * tok] = s
            for t in range(tok // HD):
                part = s[:, t * HD : (t + 1) * HD]
                mx = part if mx is None else jnp.maximum(mx, part)
        mx_ref[slot] = mx

    def finish(h, slot):
        m_old = m_in[h]
        m_new = jnp.maximum(m_old, jnp.max(mx_ref[slot], 1, keepdims=True) - row_off)
        alpha = jnp.exp2((m_old - m_new) * FACTOR)
        shift = jnp.concatenate([m_new + row_off] * (tok // HD), 1) * FACTOR
        o = None
        for k, (r, i) in enumerate(pieces):
            s = s_ref[slot, :, k * tok : (k + 1) * tok]
            p = jnp.exp2(s * FACTOR - shift).astype(BF16)
            v = jnp.concatenate([r[i + (slice(tok, 2 * tok),)], jnp.ones((tok, HD), BF16)], 1)
            d = jnp.dot(p, v, preferred_element_type=F32)
            o = d if o is None else o + d
        acc = acc_in[h] * alpha + o[:, :HD]
        total = l_in[h] * alpha + o[:, HD:]
        if last:
            outs[0][:, pl.ds(pl.multiple_of(h * HD, HD), HD)] = (acc / total).astype(BF16)
        else:
            outs[0][h] = m_new
            outs[1][h] = total
            outs[2][h] = acc

    score(0, 0)

    def step(h, _):
        score(jnp.minimum(h + 1, heads - 1), (h + 1) % 2)
        finish(h, h % 2)
        return 0

    lax.fori_loop(0, heads, step, 0)


def lay_kernel(count, *refs):
    levels, out = refs[:-1], refs[-1]
    y = lax.axis_index("ctx") % YS
    for slot in range(YS):
        for k in range(count):

            @pl.when(slot > y)
            def _():
                out[slot, k] = levels[k][...]

            @pl.when(slot <= y)
            def _():
                out[slot, k] = levels[k + 1][...]


VM = pl.BlockSpec(memory_space=pltpu.VMEM)


def params():
    return pltpu.CompilerParams(vmem_limit_bytes=40 * 2**20)


def pack(kv, docs):
    tok = kv.shape[1]
    return pl.pallas_call(
        pack_kernel,
        in_specs=[VM, VM],
        out_specs=[VM, VM],
        out_shape=[jax.ShapeDtypeStruct((2 * tok + 16, HD), BF16), jax.ShapeDtypeStruct((tok, HD), F32)],
        compiler_params=params(),
        name="pack",
    )(kv, docs)


def carry_shapes(q):
    heads, tok = q.shape[1] // HD, q.shape[0]
    return [jax.ShapeDtypeStruct((heads, tok, HD), F32)] * 3


def cost(rows, keys):
    return pl.CostEstimate(flops=4 * rows * keys * HD, bytes_accessed=4 * rows * HD, transcendentals=rows * keys)


def own(q, rows, piece):
    return pl.pallas_call(
        own_kernel,
        in_specs=[VM] * 3,
        out_specs=[VM] * 3,
        out_shape=carry_shapes(q),
        compiler_params=params(),
        cost_estimate=cost(q.size // HD, q.shape[0]),
        name="own",
    )(q, rows, piece)


def far(q, rows, pieces, carry, last):
    tok = q.shape[0]
    n = sum(p.size // (p.shape[-1] * p.shape[-2]) for p in pieces)
    return pl.pallas_call(
        functools.partial(far_kernel, last, len(pieces)),
        in_specs=[VM] * (5 + len(pieces)),
        out_specs=VM if last else [VM] * 3,
        out_shape=jax.ShapeDtypeStruct(q.shape, BF16) if last else carry_shapes(q),
        scratch_shapes=[pltpu.VMEM((2, tok, n * tok), F32), pltpu.VMEM((2, tok, HD), F32)],
        compiler_params=params(),
        cost_estimate=cost(q.size // HD, n * tok),
        name="far",
    )(q, rows, *pieces, *carry)


def lay(levels):
    count = len(levels) - 1
    return pl.pallas_call(
        functools.partial(lay_kernel, count),
        in_specs=[VM] * len(levels),
        out_specs=VM,
        out_shape=jax.ShapeDtypeStruct((YS, count, *levels[0].shape), BF16),
        compiler_params=params(),
        name="lay",
    )(*levels)


def on_device(queries, keys_values, segments):
    size = lax.axis_size("ctx")
    up = [(c, (c + YS) % size) for c in range(size)]
    groups = [list(range(c, c + YS)) for c in range(0, size, YS)]
    piece, rows = pack(keys_values, segments.reshape(-1, HD))
    levels = [piece]
    for _ in range(ROUNDS[-1][-1] + 1):
        levels.append(lax.ppermute(levels[-1], "ctx", up))
    carry = own(queries, rows, piece)
    for wanted in ROUNDS:
        sent = lay(levels[wanted[0] : wanted[-1] + 2])
        got = lax.all_to_all(sent, "ctx", 0, 0, axis_index_groups=groups)
        carry = far(queries, rows, [got], carry, wanted is ROUNDS[-1])
    return carry


def solution(mesh):
    return jax.shard_map(
        on_device,
        mesh=mesh,
        in_specs=(P("ctx", "tp"), P(None, "ctx", "tp"), P("ctx")),
        out_specs=P("ctx", "tp"),
        check_vma=False,
    )
```

```python
import functools
import itertools
import jax
import jax.numpy as jnp
from jax import lax
from jax.experimental import pallas as pl
from jax.experimental.pallas import tpu as pltpu
from jax.sharding import PartitionSpec as P

HD = 128
FAR = 1e30
FACTOR = HD ** (-0.5) * 1.4426950408889634
F32, BF16 = jnp.float32, jnp.bfloat16
NT = (((1,), (1,)), ((), ()))
YS = 4


def pack_kernel(kv_ref, docs_ref, piece_ref, rows_ref, docs_vmem, sems):
    tok = kv_ref.shape[1]
    copies = [
        pltpu.make_async_copy(docs_ref, docs_vmem, sems.at[0]),
        pltpu.make_async_copy(kv_ref.at[0], piece_ref.at[0:tok], sems.at[1]),
        pltpu.make_async_copy(kv_ref.at[1], piece_ref.at[tok : 2 * tok], sems.at[2]),
    ]
    for copy in copies:
        copy.start()
    copies[0].wait()
    docs = docs_vmem[...].astype(F32) + 1.0
    n = docs.shape[0]
    piece_ref[2 * tok :] = jnp.concatenate([docs, jnp.zeros((16 - n, HD), F32)], 0).astype(BF16)
    for t in range(n):
        rows_ref[t * HD : (t + 1) * HD] = jnp.broadcast_to(docs[t : t + 1], (HD, HD)).T
    copies[1].wait()
    copies[2].wait()


def key_docs(piece_ref, lead, tok):
    tail = piece_ref[lead + (slice(2 * tok, 2 * tok + 16),)].astype(F32)
    return jnp.concatenate([tail[t : t + 1] for t in range(tok // HD)], 1)


def own_kernel(q_ref, rows_ref, piece_ref, m_ref, l_ref, acc_ref):
    tok = q_ref.shape[0]
    keys = piece_ref[0:tok]
    values = jnp.concatenate([piece_ref[tok : 2 * tok], jnp.ones((tok, HD), BF16)], 1)
    docs = key_docs(piece_ref, (), tok)
    seen = (rows_ref[:, 0:1] == docs) & (
        lax.broadcasted_iota(jnp.int32, (tok, tok), 1) <= lax.broadcasted_iota(jnp.int32, (tok, tok), 0)
    )
    for h in range(q_ref.shape[1] // HD):
        s = lax.dot_general(q_ref[:, h * HD : (h + 1) * HD], keys, NT, preferred_element_type=F32)
        s = jnp.where(seen, s, -FAR)
        m = jnp.max(s, 1, keepdims=True)
        p = jnp.exp2((s - m) * FACTOR).astype(BF16)
        o = jnp.dot(p, values, preferred_element_type=F32)
        m_ref[h] = jnp.broadcast_to(m, (tok, HD))
        acc_ref[h] = o[:, :HD]
        l_ref[h] = o[:, HD:]


def far_kernel(last, n_refs, *refs):
    q_ref, rows_ref = refs[:2]
    piece_refs = refs[2 : 2 + n_refs]
    m_in, l_in, acc_in = refs[2 + n_refs : 5 + n_refs]
    outs = refs[5 + n_refs : -2]
    s_ref, mx_ref = refs[-2:]
    tok = q_ref.shape[0]
    heads = q_ref.shape[1] // HD
    pieces = [(r, i) for r in piece_refs for i in itertools.product(*[range(s) for s in r.shape[:-2]])]
    first = rows_ref[0:1, 0:1]
    row_off = jnp.where(rows_ref[...] == first, 0.0, FAR)
    bias = [jnp.where(key_docs(r, i, tok) == first, 0.0, -FAR) for r, i in pieces]

    def score(h, slot):
        q = q_ref[:, h * HD : (h + 1) * HD]
        mx = None
        for k, (r, i) in enumerate(pieces):
            s = lax.dot_general(q, r[i + (slice(0, tok),)], NT, preferred_element_type=F32) + bias[k]
            s_ref[slot, :, k * tok : (k + 1) * tok] = s
            for t in range(tok // HD):
                part = s[:, t * HD : (t + 1) * HD]
                mx = part if mx is None else jnp.maximum(mx, part)
        mx_ref[slot] = mx

    def finish(h, slot):
        m_old = m_in[h]
        m_new = jnp.maximum(m_old, jnp.max(mx_ref[slot], 1, keepdims=True) - row_off)
        alpha = jnp.exp2((m_old - m_new) * FACTOR)
        shift = jnp.concatenate([m_new + row_off] * (tok // HD), 1) * FACTOR
        o = None
        for k, (r, i) in enumerate(pieces):
            s = s_ref[slot, :, k * tok : (k + 1) * tok]
            p = jnp.exp2(s * FACTOR - shift).astype(BF16)
            v = jnp.concatenate([r[i + (slice(tok, 2 * tok),)], jnp.ones((tok, HD), BF16)], 1)
            d = jnp.dot(p, v, preferred_element_type=F32)
            o = d if o is None else o + d
        acc = acc_in[h] * alpha + o[:, :HD]
        total = l_in[h] * alpha + o[:, HD:]
        if last:
            outs[0][:, h * HD : (h + 1) * HD] = (acc / total).astype(BF16)
        else:
            outs[0][h] = m_new
            outs[1][h] = total
            outs[2][h] = acc

    score(0, 0)
    for h in range(heads):
        if h + 1 < heads:
            score(h + 1, (h + 1) % 2)
        finish(h, h % 2)


def lay_kernel(count, *refs):
    levels, outs = refs[: count + 1], refs[count + 1 :]
    y = lax.axis_index("ctx") % YS
    for by, out in enumerate(outs, 1):
        for k in range(count):

            @pl.when(y + by < YS)
            def _():
                out[k] = levels[k][...]

            @pl.when(y + by >= YS)
            def _():
                out[k] = levels[k + 1][...]


VM = pl.BlockSpec(memory_space=pltpu.VMEM)


def params(mib=24):
    return pltpu.CompilerParams(vmem_limit_bytes=mib * 2**20)


def pack(kv, docs):
    tok = kv.shape[1]
    return pl.pallas_call(
        pack_kernel,
        in_specs=[pl.BlockSpec(memory_space=pl.ANY)] * 2,
        out_specs=[VM, VM],
        scratch_shapes=[pltpu.VMEM(docs.shape, docs.dtype), pltpu.SemaphoreType.DMA((3,))],
        out_shape=[jax.ShapeDtypeStruct((2 * tok + 16, HD), BF16), jax.ShapeDtypeStruct((tok, HD), F32)],
        compiler_params=params(),
        name="pack",
    )(kv, docs)


def carry_shapes(q):
    heads, tok = q.shape[1] // HD, q.shape[0]
    return [jax.ShapeDtypeStruct((heads, tok, HD), F32)] * 3


def cost(rows, keys):
    return pl.CostEstimate(flops=4 * rows * keys * HD, bytes_accessed=4 * rows * HD, transcendentals=rows * keys)


def own(q, rows, piece):
    return pl.pallas_call(
        own_kernel,
        in_specs=[VM] * 3,
        out_specs=[VM] * 3,
        out_shape=carry_shapes(q),
        compiler_params=params(),
        cost_estimate=cost(q.size // HD, q.shape[0]),
        name="own",
    )(q, rows, piece)


def far(q, rows, pieces, carry, last):
    tok = q.shape[0]
    n = sum(p.size // (p.shape[-1] * p.shape[-2]) for p in pieces)
    return pl.pallas_call(
        functools.partial(far_kernel, last, len(pieces)),
        in_specs=[VM] * (5 + len(pieces)),
        out_specs=VM if last else [VM] * 3,
        out_shape=jax.ShapeDtypeStruct(q.shape, BF16) if last else carry_shapes(q),
        scratch_shapes=[pltpu.VMEM((2, tok, n * tok), F32), pltpu.VMEM((2, tok, HD), F32)],
        compiler_params=params(),
        cost_estimate=cost(q.size // HD, n * tok),
        name="far",
    )(q, rows, *pieces, *carry)


def lay(levels):
    count = len(levels) - 1
    return pl.pallas_call(
        functools.partial(lay_kernel, count),
        in_specs=[VM] * len(levels),
        out_specs=[VM] * (YS - 1),
        out_shape=[jax.ShapeDtypeStruct((count, *levels[0].shape), BF16)] * (YS - 1),
        compiler_params=params(),
        name="lay",
    )(*levels)


def on_device(queries, keys_values, segments):
    size = lax.axis_size("ctx")

    def up(x, by):
        return lax.ppermute(x, "ctx", [(c, c + by * YS) for c in range(size - by * YS)])

    def across(x, by):
        return lax.ppermute(x, "ctx", [(c, c - c % YS + (c + by) % YS) for c in range(size)])

    piece, rows = pack(keys_values, segments.reshape(-1, HD))
    two = up(piece, 2)
    one = up(piece, 1)
    carry = own(queries, rows, piece)
    two, carry = lax.optimization_barrier((two, carry))
    both = up(jnp.stack([one, two]), 2)
    near = [across(x, by) for by, x in enumerate(lay([piece, one, two]), 1)]
    carry = far(queries, rows, [one, two], carry, False)
    both, carry = lax.optimization_barrier((both, carry))
    away = [across(x, by) for by, x in enumerate(lay([two, both[0], both[1]]), 1)]
    carry = far(queries, rows, [both, *near], carry, False)
    carry = far(queries, rows, [away[0], away[2]], carry, False)
    return far(queries, rows, [away[1]], carry, True)


def solution(mesh):
    return jax.shard_map(
        on_device,
        mesh=mesh,
        in_specs=(P("ctx", "tp"), P(None, "ctx", "tp"), P("ctx")),
        out_specs=P("ctx", "tp"),
        check_vma=False,
    )
```

```python
import functools
import jax
import jax.numpy as jnp
from jax import lax
from jax.experimental import pallas as pl
from jax.experimental.pallas import tpu as pltpu
from jax.sharding import PartitionSpec as P

HD = 128
FAR = 1e30
FACTOR = HD ** (-0.5) * 1.4426950408889634
F32, BF16 = jnp.float32, jnp.bfloat16
NT = (((1,), (1,)), ((), ()))
YS = 4


def pack_kernel(kv_ref, docs_ref, piece_ref, rows_ref, docs_vmem, sems):
    tok = kv_ref.shape[1]
    copies = [
        pltpu.make_async_copy(docs_ref, docs_vmem, sems.at[0]),
        pltpu.make_async_copy(kv_ref.at[0], piece_ref.at[0:tok], sems.at[1]),
        pltpu.make_async_copy(kv_ref.at[1], piece_ref.at[tok : 2 * tok], sems.at[2]),
    ]
    for copy in copies:
        copy.start()
    copies[0].wait()
    docs = docs_vmem[...].astype(F32) + 1.0
    n = docs.shape[0]
    piece_ref[2 * tok :] = jnp.concatenate([docs, jnp.zeros((16 - n, HD), F32)], 0).astype(BF16)
    for t in range(n):
        rows_ref[t * HD : (t + 1) * HD] = jnp.broadcast_to(docs[t : t + 1], (HD, HD)).T
    copies[1].wait()
    copies[2].wait()


def key_docs(piece_ref, lead, tok):
    tail = piece_ref[lead + (slice(2 * tok, 2 * tok + 16),)].astype(F32)
    return jnp.concatenate([tail[t : t + 1] for t in range(tok // HD)], 1)


def own_kernel(q_ref, rows_ref, piece_ref, m_ref, l_ref, acc_ref):
    tok = q_ref.shape[0]
    keys = piece_ref[0:tok]
    values = jnp.concatenate([piece_ref[tok : 2 * tok], jnp.ones((tok, HD), BF16)], 1)
    docs = key_docs(piece_ref, (), tok)
    seen = (rows_ref[:, 0:1] == docs) & (
        lax.broadcasted_iota(jnp.int32, (tok, tok), 1) <= lax.broadcasted_iota(jnp.int32, (tok, tok), 0)
    )
    for h in range(q_ref.shape[1] // HD):
        s = lax.dot_general(q_ref[:, h * HD : (h + 1) * HD], keys, NT, preferred_element_type=F32)
        s = jnp.where(seen, s, -FAR)
        m = jnp.max(s, 1, keepdims=True)
        p = jnp.exp2((s - m) * FACTOR).astype(BF16)
        o = jnp.dot(p, values, preferred_element_type=F32)
        m_ref[h] = jnp.broadcast_to(m, (tok, HD))
        acc_ref[h] = o[:, :HD]
        l_ref[h] = o[:, HD:]


def far_kernel(last, tiers, n_refs, *refs):
    q_ref, rows_ref = refs[:2]
    piece_refs = refs[2 : 2 + n_refs]
    carry_in = refs[2 + n_refs : 5 + n_refs]
    m_in, l_in, acc_in = carry_in
    if last:
        out_hbm, s_ref, mx_ref, result, sems = refs[5 + n_refs :]
    else:
        *outs, s_ref, mx_ref = refs[5 + n_refs :]
    tok = q_ref.shape[0]
    heads = q_ref.shape[1] // HD
    first = rows_ref[0:1, 0:1]

    def leave(h):
        columns = slice(h * HD, (h + 1) * HD)
        return pltpu.make_async_copy(result.at[:, columns], out_hbm.at[:, columns], sems.at[h])

    def attend(pieces, bias):
        row_off = jnp.where(rows_ref[...] == first, 0.0, FAR)

        def score(h, slot):
            q = q_ref[:, h * HD : (h + 1) * HD]
            mx = None
            for k, (r, i) in enumerate(pieces):
                s = lax.dot_general(q, r[i + (slice(0, tok),)], NT, preferred_element_type=F32) + bias[k]
                s_ref[slot, :, k * tok : (k + 1) * tok] = s
                for t in range(tok // HD):
                    part = s[:, t * HD : (t + 1) * HD]
                    mx = part if mx is None else jnp.maximum(mx, part)
            mx_ref[slot] = mx

        def finish(h, slot):
            m_old = m_in[h]
            m_new = jnp.maximum(m_old, jnp.max(mx_ref[slot], 1, keepdims=True) - row_off)
            alpha = jnp.exp2((m_old - m_new) * FACTOR)
            shift = jnp.concatenate([m_new + row_off] * (tok // HD), 1) * FACTOR
            o = None
            for k, (r, i) in enumerate(pieces):
                s = s_ref[slot, :, k * tok : (k + 1) * tok]
                p = jnp.exp2(s * FACTOR - shift).astype(BF16)
                v = jnp.concatenate([r[i + (slice(tok, 2 * tok),)], jnp.ones((tok, HD), BF16)], 1)
                d = jnp.dot(p, v, preferred_element_type=F32)
                o = d if o is None else o + d
            acc = acc_in[h] * alpha + o[:, :HD]
            total = l_in[h] * alpha + o[:, HD:]
            if last:
                result[:, h * HD : (h + 1) * HD] = (acc / total).astype(BF16)
                leave(h).start()
            else:
                outs[0][h] = m_new
                outs[1][h] = total
                outs[2][h] = acc

        score(0, 0)
        for h in range(heads):
            if h + 1 < heads:
                score(h + 1, (h + 1) % 2)
            finish(h, h % 2)

    pieces, bias, seen = [], [], []
    for tier in tiers:
        new = [(piece_refs[n], i) for n, i in tier]
        pieces.append((pieces[-1] if pieces else []) + new)
        new_bias = [jnp.where(key_docs(r, i, tok) == first, 0.0, -FAR) for r, i in new]
        bias.append((bias[-1] if bias else []) + new_bias)
        seen.append(jnp.max(functools.reduce(jnp.maximum, new_bias)) == 0.0)

    farther = jnp.bool_(False)
    for t in reversed(range(len(tiers))):

        @pl.when(seen[t] & jnp.logical_not(farther))
        def _():
            attend(pieces[t], bias[t])

        farther = farther | seen[t]

    @pl.when(jnp.logical_not(farther))
    def _():
        for h in range(heads):
            if last:
                result[:, h * HD : (h + 1) * HD] = (acc_in[h] / l_in[h]).astype(BF16)
                leave(h).start()
            else:
                for ref, out in zip(carry_in, outs):
                    out[h] = ref[h]

    if last:
        for h in range(heads):
            leave(h).wait()


def lay_kernel(count, *refs):
    levels, outs = refs[: count + 1], refs[count + 1 :]
    y = lax.axis_index("ctx") % YS
    for by, out in enumerate(outs, 1):
        for k in range(count):

            @pl.when(y + by < YS)
            def _():
                out[k] = levels[k][...]

            @pl.when(y + by >= YS)
            def _():
                out[k] = levels[k + 1][...]


VM = pl.BlockSpec(memory_space=pltpu.VMEM)
HBM = pl.BlockSpec(memory_space=pltpu.HBM)


def params(mib=24):
    return pltpu.CompilerParams(vmem_limit_bytes=mib * 2**20)


def pack(kv, docs):
    tok = kv.shape[1]
    return pl.pallas_call(
        pack_kernel,
        in_specs=[pl.BlockSpec(memory_space=pl.ANY)] * 2,
        out_specs=[VM, VM],
        scratch_shapes=[pltpu.VMEM(docs.shape, docs.dtype), pltpu.SemaphoreType.DMA((3,))],
        out_shape=[jax.ShapeDtypeStruct((2 * tok + 16, HD), BF16), jax.ShapeDtypeStruct((tok, HD), F32)],
        compiler_params=params(),
        name="pack",
    )(kv, docs)


def carry_shapes(q):
    heads, tok = q.shape[1] // HD, q.shape[0]
    return [jax.ShapeDtypeStruct((heads, tok, HD), F32)] * 3


def cost(rows, keys):
    return pl.CostEstimate(flops=4 * rows * keys * HD, bytes_accessed=4 * rows * HD, transcendentals=rows * keys)


def own(q, rows, piece):
    return pl.pallas_call(
        own_kernel,
        in_specs=[VM] * 3,
        out_specs=[VM] * 3,
        out_shape=carry_shapes(q),
        compiler_params=params(),
        cost_estimate=cost(q.size // HD, q.shape[0]),
        name="own",
    )(q, rows, piece)


def far(q, rows, pieces, tiers, carry, last):
    tok = q.shape[0]
    n = sum(map(len, tiers))
    return pl.pallas_call(
        functools.partial(far_kernel, last, tiers, len(pieces)),
        in_specs=[VM] * (5 + len(pieces)),
        out_specs=HBM if last else [VM] * 3,
        out_shape=jax.ShapeDtypeStruct(q.shape, BF16) if last else carry_shapes(q),
        scratch_shapes=[pltpu.VMEM((2, tok, n * tok), F32), pltpu.VMEM((2, tok, HD), F32)]
        + [pltpu.VMEM(q.shape, BF16), pltpu.SemaphoreType.DMA((q.shape[1] // HD,))] * last,
        compiler_params=params(),
        cost_estimate=cost(q.size // HD, n * tok),
        name="far",
    )(q, rows, *pieces, *carry)


def lay(levels):
    count = len(levels) - 1
    return pl.pallas_call(
        functools.partial(lay_kernel, count),
        in_specs=[VM] * len(levels),
        out_specs=[VM] * (YS - 1),
        out_shape=[jax.ShapeDtypeStruct((count, *levels[0].shape), BF16)] * (YS - 1),
        compiler_params=params(),
        name="lay",
    )(*levels)


def on_device(queries, keys_values, segments):
    size = lax.axis_size("ctx")

    def up(x, by):
        return lax.ppermute(x, "ctx", [(c, c + by * YS) for c in range(size - by * YS)])

    def across(x, by):
        return lax.ppermute(x, "ctx", [(c, c - c % YS + (c + by) % YS) for c in range(size)])

    piece, rows = pack(keys_values, segments.reshape(-1, HD))
    two = up(piece, 2)
    one = up(piece, 1)
    carry = own(queries, rows, piece)
    two, carry = lax.optimization_barrier((two, carry))
    both = up(jnp.stack([one, two]), 2)
    near = [across(x, by) for by, x in enumerate(lay([piece, one, two]), 1)]
    carry = far(queries, rows, [one, two], [[(0, ()), (1, ())]], carry, False)
    both, carry = lax.optimization_barrier((both, carry))
    away = [across(x, by) for by, x in enumerate(lay([two, both[0], both[1]]), 1)]
    carry = far(
        queries,
        rows,
        [*near, both],
        [[(0, (0,)), (1, (0,)), (2, (0,))], [(0, (1,)), (1, (1,)), (2, (1,)), (3, (0,)), (3, (1,))]],
        carry,
        False,
    )
    carry = far(queries, rows, [away[1]], [[(0, (0,)), (0, (1,))]], carry, False)
    ends = [[(0, (0,)), (1, (0,)), (0, (1,)), (1, (1,))]]
    return far(queries, rows, [away[0], away[2]], ends, carry, True)


def solution(mesh):
    return jax.shard_map(
        on_device,
        mesh=mesh,
        in_specs=(P("ctx", "tp"), P(None, "ctx", "tp"), P("ctx")),
        out_specs=P("ctx", "tp"),
        check_vma=False,
    )
```

```python
import functools
import jax
import jax.numpy as jnp
from jax import lax
from jax.experimental import pallas as pl
from jax.experimental.pallas import tpu as pltpu
from jax.sharding import PartitionSpec as P

HD = 128
FAR = 1e30
FACTOR = HD ** (-0.5) * 1.4426950408889634
F32, BF16 = jnp.float32, jnp.bfloat16
NT = (((1,), (1,)), ((), ()))
YS = 4


def pack_kernel(kv_ref, docs_ref, piece_ref, rows_ref):
    tok = kv_ref.shape[1]
    piece_ref[0:tok] = kv_ref[0]
    piece_ref[tok : 2 * tok] = kv_ref[1]
    docs = docs_ref[...].astype(F32) + 1.0
    n = docs.shape[0]
    piece_ref[2 * tok :] = jnp.concatenate([docs, jnp.zeros((16 - n, HD), F32)], 0).astype(BF16)
    for t in range(n):
        rows_ref[t * HD : (t + 1) * HD] = jnp.broadcast_to(docs[t : t + 1], (HD, HD)).T


def key_docs(piece_ref, lead, tok):
    tail = piece_ref[lead + (slice(2 * tok, 2 * tok + 16),)].astype(F32)
    return jnp.concatenate([tail[t : t + 1] for t in range(tok // HD)], 1)


def own_kernel(q_ref, rows_ref, piece_ref, m_ref, l_ref, acc_ref):
    tok = q_ref.shape[0]
    keys = piece_ref[0:tok]
    values = jnp.concatenate([piece_ref[tok : 2 * tok], jnp.ones((tok, HD), BF16)], 1)
    docs = key_docs(piece_ref, (), tok)
    seen = (rows_ref[:, 0:1] == docs) & (
        lax.broadcasted_iota(jnp.int32, (tok, tok), 1) <= lax.broadcasted_iota(jnp.int32, (tok, tok), 0)
    )
    for h in range(q_ref.shape[1] // HD):
        s = lax.dot_general(q_ref[:, h * HD : (h + 1) * HD], keys, NT, preferred_element_type=F32)
        s = jnp.where(seen, s, -FAR)
        m = jnp.max(s, 1, keepdims=True)
        p = jnp.exp2((s - m) * FACTOR).astype(BF16)
        o = jnp.dot(p, values, preferred_element_type=F32)
        m_ref[h] = jnp.broadcast_to(m, (tok, HD))
        acc_ref[h] = o[:, :HD]
        l_ref[h] = o[:, HD:]


def far_kernel(last, tiers, n_refs, *refs):
    q_ref, rows_ref = refs[:2]
    piece_refs = refs[2 : 2 + n_refs]
    carry_in = refs[2 + n_refs : 5 + n_refs]
    m_in, l_in, acc_in = carry_in
    if last:
        out_hbm, s_ref, mx_ref, result, sems = refs[5 + n_refs :]
    else:
        *outs, s_ref, mx_ref = refs[5 + n_refs :]
    tok = q_ref.shape[0]
    heads = q_ref.shape[1] // HD
    first = rows_ref[0:1, 0:1]

    def leave(h):
        columns = slice(h * HD, (h + 1) * HD)
        return pltpu.make_async_copy(result.at[:, columns], out_hbm.at[:, columns], sems.at[h])

    def attend(pieces, bias):
        row_off = jnp.where(rows_ref[...] == first, 0.0, FAR)

        def score(h, slot):
            q = q_ref[:, h * HD : (h + 1) * HD]
            mx = None
            for k, (r, i) in enumerate(pieces):
                s = lax.dot_general(q, r[i + (slice(0, tok),)], NT, preferred_element_type=F32) + bias[k]
                s_ref[slot, :, k * tok : (k + 1) * tok] = s
                for t in range(tok // HD):
                    part = s[:, t * HD : (t + 1) * HD]
                    mx = part if mx is None else jnp.maximum(mx, part)
            mx_ref[slot] = mx

        def finish(h, slot):
            m_old = m_in[h]
            m_new = jnp.maximum(m_old, jnp.max(mx_ref[slot], 1, keepdims=True) - row_off)
            alpha = jnp.exp2((m_old - m_new) * FACTOR)
            shift = jnp.concatenate([m_new + row_off] * (tok // HD), 1) * FACTOR
            o = None
            for k, (r, i) in enumerate(pieces):
                s = s_ref[slot, :, k * tok : (k + 1) * tok]
                p = jnp.exp2(s * FACTOR - shift).astype(BF16)
                v = jnp.concatenate([r[i + (slice(tok, 2 * tok),)], jnp.ones((tok, HD), BF16)], 1)
                d = jnp.dot(p, v, preferred_element_type=F32)
                o = d if o is None else o + d
            acc = acc_in[h] * alpha + o[:, :HD]
            total = l_in[h] * alpha + o[:, HD:]
            if last:
                result[:, h * HD : (h + 1) * HD] = (acc / total).astype(BF16)
                leave(h).start()
            else:
                outs[0][h] = m_new
                outs[1][h] = total
                outs[2][h] = acc

        score(0, 0)
        for h in range(heads):
            if h + 1 < heads:
                score(h + 1, (h + 1) % 2)
            finish(h, h % 2)

    pieces, bias, seen = [], [], []
    for tier in tiers:
        new = [(piece_refs[n], i) for n, i in tier]
        pieces.append((pieces[-1] if pieces else []) + new)
        new_bias = [jnp.where(key_docs(r, i, tok) == first, 0.0, -FAR) for r, i in new]
        bias.append((bias[-1] if bias else []) + new_bias)
        seen.append(jnp.max(functools.reduce(jnp.maximum, new_bias)) == 0.0)

    farther = jnp.bool_(False)
    for t in reversed(range(len(tiers))):

        @pl.when(seen[t] & jnp.logical_not(farther))
        def _():
            attend(pieces[t], bias[t])

        farther = farther | seen[t]

    @pl.when(jnp.logical_not(farther))
    def _():
        for h in range(heads):
            if last:
                result[:, h * HD : (h + 1) * HD] = (acc_in[h] / l_in[h]).astype(BF16)
                leave(h).start()
            else:
                for ref, out in zip(carry_in, outs):
                    out[h] = ref[h]

    if last:
        for h in range(heads):
            leave(h).wait()


def lay_kernel(count, *refs):
    levels, outs = refs[: count + 1], refs[count + 1 :]
    y = lax.axis_index("ctx") % YS
    for by, out in enumerate(outs, 1):
        for k in range(count):

            @pl.when(y + by < YS)
            def _():
                out[k] = levels[k][...]

            @pl.when(y + by >= YS)
            def _():
                out[k] = levels[k + 1][...]


VM = pl.BlockSpec(memory_space=pltpu.VMEM)
HBM = pl.BlockSpec(memory_space=pltpu.HBM)


def params(mib=24):
    return pltpu.CompilerParams(vmem_limit_bytes=mib * 2**20)


def pack(kv, docs):
    tok = kv.shape[1]
    return pl.pallas_call(
        pack_kernel,
        grid=(1,),
        in_specs=[pl.BlockSpec(kv.shape, lambda i: (0, 0, 0)), pl.BlockSpec(docs.shape, lambda i: (0, 0))],
        out_specs=[VM, VM],
        out_shape=[jax.ShapeDtypeStruct((2 * tok + 16, HD), BF16), jax.ShapeDtypeStruct((tok, HD), F32)],
        compiler_params=params(),
        name="pack",
    )(kv, docs)


def carry_shapes(q):
    heads, tok = q.shape[1] // HD, q.shape[0]
    return [jax.ShapeDtypeStruct((heads, tok, HD), F32)] * 3


def cost(rows, keys):
    return pl.CostEstimate(flops=4 * rows * keys * HD, bytes_accessed=4 * rows * HD, transcendentals=rows * keys)


def own(q, rows, piece):
    return pl.pallas_call(
        own_kernel,
        in_specs=[VM] * 3,
        out_specs=[VM] * 3,
        out_shape=carry_shapes(q),
        compiler_params=params(),
        cost_estimate=cost(q.size // HD, q.shape[0]),
        name="own",
    )(q, rows, piece)


def far(q, rows, pieces, tiers, carry, last):
    tok = q.shape[0]
    n = sum(map(len, tiers))
    return pl.pallas_call(
        functools.partial(far_kernel, last, tiers, len(pieces)),
        in_specs=[VM] * (5 + len(pieces)),
        out_specs=HBM if last else [VM] * 3,
        out_shape=jax.ShapeDtypeStruct(q.shape, BF16) if last else carry_shapes(q),
        scratch_shapes=[pltpu.VMEM((2, tok, n * tok), F32), pltpu.VMEM((2, tok, HD), F32)]
        + [pltpu.VMEM(q.shape, BF16), pltpu.SemaphoreType.DMA((q.shape[1] // HD,))] * last,
        compiler_params=params(),
        cost_estimate=cost(q.size // HD, n * tok),
        name="far",
    )(q, rows, *pieces, *carry)


def lay(levels):
    count = len(levels) - 1
    return pl.pallas_call(
        functools.partial(lay_kernel, count),
        in_specs=[VM] * len(levels),
        out_specs=[VM] * (YS - 1),
        out_shape=[jax.ShapeDtypeStruct((count, *levels[0].shape), BF16)] * (YS - 1),
        compiler_params=params(),
        name="lay",
    )(*levels)


def on_device(queries, keys_values, segments):
    size = lax.axis_size("ctx")

    def up(x, by):
        return lax.ppermute(x, "ctx", [(c, c + by * YS) for c in range(size - by * YS)])

    def across(x, by):
        return lax.ppermute(x, "ctx", [(c, c - c % YS + (c + by) % YS) for c in range(size)])

    piece, rows = pack(keys_values, segments.reshape(-1, HD))
    two = up(piece, 2)
    one = up(piece, 1)
    carry = own(queries, rows, piece)
    two, carry = lax.optimization_barrier((two, carry))
    both = up(jnp.stack([one, two]), 2)
    near = [across(x, by) for by, x in enumerate(lay([piece, one, two]), 1)]
    carry = far(queries, rows, [one, two], [[(0, ()), (1, ())]], carry, False)
    both, carry = lax.optimization_barrier((both, carry))
    away = [across(x, by) for by, x in enumerate(lay([two, both[0], both[1]]), 1)]
    carry = far(
        queries,
        rows,
        [near[1], near[0], near[2], both],
        [[(0, (0,)), (1, (0,)), (2, (0,))], [(0, (1,)), (1, (1,)), (2, (1,)), (3, (0,)), (3, (1,))]],
        carry,
        False,
    )
    carry = far(queries, rows, [away[1]], [[(0, (0,)), (0, (1,))]], carry, False)
    ends = [[(0, (0,)), (1, (0,)), (0, (1,)), (1, (1,))]]
    return far(queries, rows, [away[0], away[2]], ends, carry, True)


def solution(mesh):
    return jax.shard_map(
        on_device,
        mesh=mesh,
        in_specs=(P("ctx", "tp"), P(None, "ctx", "tp"), P("ctx")),
        out_specs=P("ctx", "tp"),
        check_vma=False,
    )
```

```python
import functools
import jax
import jax.numpy as jnp
from jax import lax
from jax.experimental import pallas as pl
from jax.experimental.pallas import tpu as pltpu
from jax.sharding import PartitionSpec as P

HD = 128
FAR = 1e30
FACTOR = HD ** (-0.5) * 1.4426950408889634
F32, BF16 = jnp.float32, jnp.bfloat16
NT = (((1,), (1,)), ((), ()))
YS = 4


def pack_kernel(kv_ref, docs_ref, piece_ref, rows_ref):
    tok = kv_ref.shape[1]
    piece_ref[0:tok] = kv_ref[0]
    piece_ref[tok : 2 * tok] = kv_ref[1]
    docs = docs_ref[...].astype(F32) + 1.0
    n = docs.shape[0]
    piece_ref[2 * tok :] = jnp.concatenate([docs, jnp.zeros((16 - n, HD), F32)], 0).astype(BF16)
    for t in range(n):
        rows_ref[t * HD : (t + 1) * HD] = jnp.broadcast_to(docs[t : t + 1], (HD, HD)).T


def key_docs(piece_ref, lead, tok):
    tail = piece_ref[lead + (slice(2 * tok, 2 * tok + 16),)].astype(F32)
    return jnp.concatenate([tail[t : t + 1] for t in range(tok // HD)], 1)


def own_kernel(q_ref, rows_ref, piece_ref, m_ref, l_ref, acc_ref):
    tok = q_ref.shape[0]
    keys = piece_ref[0:tok]
    values = jnp.concatenate([piece_ref[tok : 2 * tok], jnp.ones((tok, HD), BF16)], 1)
    docs = key_docs(piece_ref, (), tok)
    seen = (rows_ref[:, 0:1] == docs) & (
        lax.broadcasted_iota(jnp.int32, (tok, tok), 1) <= lax.broadcasted_iota(jnp.int32, (tok, tok), 0)
    )
    for h in range(q_ref.shape[1] // HD):
        s = lax.dot_general(q_ref[:, h * HD : (h + 1) * HD], keys, NT, preferred_element_type=F32)
        s = jnp.where(seen, s, -FAR)
        m = jnp.max(s, 1, keepdims=True)
        p = jnp.exp2((s - m) * FACTOR).astype(BF16)
        o = jnp.dot(p, values, preferred_element_type=F32)
        m_ref[h] = jnp.broadcast_to(m, (tok, HD))
        acc_ref[h] = o[:, :HD]
        l_ref[h] = o[:, HD:]


def far_kernel(last, tiers, n_refs, *refs):
    q_ref, rows_ref = refs[:2]
    piece_refs = refs[2 : 2 + n_refs]
    carry_in = refs[2 + n_refs : 5 + n_refs]
    m_in, l_in, acc_in = carry_in
    if last:
        out_hbm, s_ref, mx_ref, result, sems = refs[5 + n_refs :]
    else:
        *outs, s_ref, mx_ref = refs[5 + n_refs :]
    tok = q_ref.shape[0]
    heads = q_ref.shape[1] // HD
    first = rows_ref[0:1, 0:1]

    def leave(h):
        columns = slice(h * HD, (h + 1) * HD)
        return pltpu.make_async_copy(result.at[:, columns], out_hbm.at[:, columns], sems.at[h])

    def attend(pieces, bias):
        row_off = jnp.where(rows_ref[...] == first, 0.0, FAR)

        def score(h, slot):
            q = q_ref[:, h * HD : (h + 1) * HD]
            mx = None
            for k, (r, i) in enumerate(pieces):
                s = lax.dot_general(q, r[i + (slice(0, tok),)], NT, preferred_element_type=F32) + bias[k]
                s_ref[slot, :, k * tok : (k + 1) * tok] = s
                for t in range(tok // HD):
                    part = s[:, t * HD : (t + 1) * HD]
                    mx = part if mx is None else jnp.maximum(mx, part)
            mx_ref[slot] = mx

        def finish(h, slot):
            m_old = m_in[h]
            m_new = jnp.maximum(m_old, jnp.max(mx_ref[slot], 1, keepdims=True) - row_off)
            alpha = jnp.exp2((m_old - m_new) * FACTOR)
            shift = jnp.concatenate([m_new + row_off] * (tok // HD), 1) * FACTOR
            o = None
            for k, (r, i) in enumerate(pieces):
                s = s_ref[slot, :, k * tok : (k + 1) * tok]
                p = jnp.exp2(s * FACTOR - shift).astype(BF16)
                v = jnp.concatenate([r[i + (slice(tok, 2 * tok),)], jnp.ones((tok, HD), BF16)], 1)
                d = jnp.dot(p, v, preferred_element_type=F32)
                o = d if o is None else o + d
            acc = acc_in[h] * alpha + o[:, :HD]
            total = l_in[h] * alpha + o[:, HD:]
            if last:
                result[:, h * HD : (h + 1) * HD] = (acc / total).astype(BF16)
                leave(h).start()
            else:
                outs[0][h] = m_new
                outs[1][h] = total
                outs[2][h] = acc

        score(0, 0)
        for h in range(heads):
            if h + 1 < heads:
                score(h + 1, (h + 1) % 2)
            finish(h, h % 2)

    pieces, bias, seen = [], [], []
    for tier in tiers:
        new = [(piece_refs[n], i) for n, i in tier]
        pieces.append((pieces[-1] if pieces else []) + new)
        new_bias = [jnp.where(key_docs(r, i, tok) == first, 0.0, -FAR) for r, i in new]
        bias.append((bias[-1] if bias else []) + new_bias)
        seen.append(jnp.max(functools.reduce(jnp.maximum, new_bias)) == 0.0)

    farther = jnp.bool_(False)
    for t in reversed(range(len(tiers))):

        @pl.when(seen[t] & jnp.logical_not(farther))
        def _():
            attend(pieces[t], bias[t])

        farther = farther | seen[t]

    @pl.when(jnp.logical_not(farther))
    def _():
        for h in range(heads):
            if last:
                result[:, h * HD : (h + 1) * HD] = (acc_in[h] / l_in[h]).astype(BF16)
                leave(h).start()
            else:
                for ref, out in zip(carry_in, outs):
                    out[h] = ref[h]

    if last:
        for h in range(heads):
            leave(h).wait()


def lay_kernel(count, *refs):
    levels, outs = refs[: count + 1], refs[count + 1 :]
    y = lax.axis_index("ctx") % YS
    for by, out in enumerate(outs, 1):
        for k in range(count):

            @pl.when(y + by < YS)
            def _():
                out[k] = levels[k][...]

            @pl.when(y + by >= YS)
            def _():
                out[k] = levels[k + 1][...]


VM = pl.BlockSpec(memory_space=pltpu.VMEM)
HBM = pl.BlockSpec(memory_space=pltpu.HBM)


def params(mib=24):
    return pltpu.CompilerParams(vmem_limit_bytes=mib * 2**20)


def pack(kv, docs):
    tok = kv.shape[1]
    return pl.pallas_call(
        pack_kernel,
        grid=(1,),
        in_specs=[pl.BlockSpec(kv.shape, lambda i: (0, 0, 0)), pl.BlockSpec(docs.shape, lambda i: (0, 0))],
        out_specs=[VM, VM],
        out_shape=[jax.ShapeDtypeStruct((2 * tok + 16, HD), BF16), jax.ShapeDtypeStruct((tok, HD), F32)],
        compiler_params=params(),
        name="pack",
    )(kv, docs)


def carry_shapes(q):
    heads, tok = q.shape[1] // HD, q.shape[0]
    return [jax.ShapeDtypeStruct((heads, tok, HD), F32)] * 3


def cost(rows, keys):
    return pl.CostEstimate(flops=4 * rows * keys * HD, bytes_accessed=4 * rows * HD, transcendentals=rows * keys)


def own(q, rows, piece):
    return pl.pallas_call(
        own_kernel,
        in_specs=[VM] * 3,
        out_specs=[VM] * 3,
        out_shape=carry_shapes(q),
        compiler_params=params(),
        cost_estimate=cost(q.size // HD, q.shape[0]),
        name="own",
    )(q, rows, piece)


def far(q, rows, pieces, tiers, carry, last):
    tok = q.shape[0]
    n = sum(map(len, tiers))
    return pl.pallas_call(
        functools.partial(far_kernel, last, tiers, len(pieces)),
        in_specs=[VM] * (5 + len(pieces)),
        out_specs=HBM if last else [VM] * 3,
        out_shape=jax.ShapeDtypeStruct(q.shape, BF16) if last else carry_shapes(q),
        scratch_shapes=[pltpu.VMEM((2, tok, n * tok), F32), pltpu.VMEM((2, tok, HD), F32)]
        + [pltpu.VMEM(q.shape, BF16), pltpu.SemaphoreType.DMA((q.shape[1] // HD,))] * last,
        compiler_params=params(),
        cost_estimate=cost(q.size // HD, n * tok),
        name="far",
    )(q, rows, *pieces, *carry)


def lay(levels):
    count = len(levels) - 1
    return pl.pallas_call(
        functools.partial(lay_kernel, count),
        in_specs=[VM] * len(levels),
        out_specs=[VM] * (YS - 1),
        out_shape=[jax.ShapeDtypeStruct((count, *levels[0].shape), BF16)] * (YS - 1),
        compiler_params=params(),
        name="lay",
    )(*levels)


def on_device(queries, keys_values, segments):
    size = lax.axis_size("ctx")

    def up(x, by):
        return lax.ppermute(x, "ctx", [(c, c + by * YS) for c in range(size - by * YS)])

    def across(x, by):
        return lax.ppermute(x, "ctx", [(c, c - c % YS + (c + by) % YS) for c in range(size)])

    piece, rows = pack(keys_values, segments.reshape(-1, HD))
    two = up(piece, 2)
    one = up(piece, 1)
    carry = own(queries, rows, piece)
    two, carry = lax.optimization_barrier((two, carry))
    both = up(jnp.stack([one, two]), 2)
    near = [across(x, by) for by, x in enumerate(lay([piece, one, two]), 1)]
    carry = far(queries, rows, [one, two], [[(0, ()), (1, ())]], carry, False)
    both, carry = lax.optimization_barrier((both, carry))
    away = [across(x, by) for by, x in enumerate(lay([two, both[0], both[1]]), 1)]
    carry = far(
        queries,
        rows,
        [near[1], near[0], near[2], both],
        [[(0, (0,)), (1, (0,)), (2, (0,))], [(0, (1,)), (1, (1,)), (2, (1,)), (3, (0,)), (3, (1,))]],
        carry,
        False,
    )
    carry = far(queries, rows, [away[1]], [[(0, (0,)), (0, (1,))]], carry, False)
    two_rows = [[(0, (0,)), (0, (1,))]]
    carry = far(queries, rows, [away[2]], two_rows, carry, False)
    return far(queries, rows, [away[0]], two_rows, carry, True)


def solution(mesh):
    return jax.shard_map(
        on_device,
        mesh=mesh,
        in_specs=(P("ctx", "tp"), P(None, "ctx", "tp"), P("ctx")),
        out_specs=P("ctx", "tp"),
        check_vma=False,
    )
```

```python
import functools
import jax
import jax.numpy as jnp
from jax import lax
from jax.experimental import pallas as pl
from jax.experimental.pallas import tpu as pltpu
from jax.sharding import PartitionSpec as P

HD = 128
FAR = 1e30
FACTOR = HD ** (-0.5) * 1.4426950408889634
F32, BF16 = jnp.float32, jnp.bfloat16
NT = (((1,), (1,)), ((), ()))
YS = 4


def pack_kernel(kv_ref, docs_ref, piece_ref, rows_ref):
    tok = kv_ref.shape[1]
    piece_ref[0:tok] = kv_ref[0]
    piece_ref[tok : 2 * tok] = kv_ref[1]
    docs = docs_ref[...].astype(F32) + 1.0
    n = docs.shape[0]
    piece_ref[2 * tok :] = jnp.concatenate([docs, jnp.zeros((16 - n, HD), F32)], 0).astype(BF16)
    for t in range(n):
        rows_ref[t * HD : (t + 1) * HD] = jnp.broadcast_to(docs[t : t + 1], (HD, HD)).T


def key_docs(piece_ref, lead, tok):
    tail = piece_ref[lead + (slice(2 * tok, 2 * tok + 16),)].astype(F32)
    return jnp.concatenate([tail[t : t + 1] for t in range(tok // HD)], 1)


def own_kernel(q_ref, rows_ref, piece_ref, m_ref, l_ref, acc_ref):
    tok = q_ref.shape[0]
    keys = piece_ref[0:tok]
    values = jnp.concatenate([piece_ref[tok : 2 * tok], jnp.ones((tok, HD), BF16)], 1)
    docs = key_docs(piece_ref, (), tok)
    seen = (rows_ref[:, 0:1] == docs) & (
        lax.broadcasted_iota(jnp.int32, (tok, tok), 1) <= lax.broadcasted_iota(jnp.int32, (tok, tok), 0)
    )
    for h in range(q_ref.shape[1] // HD):
        s = lax.dot_general(q_ref[:, h * HD : (h + 1) * HD], keys, NT, preferred_element_type=F32)
        s = jnp.where(seen, s, -FAR)
        m = jnp.max(s, 1, keepdims=True)
        p = jnp.exp2((s - m) * FACTOR).astype(BF16)
        o = jnp.dot(p, values, preferred_element_type=F32)
        m_ref[h] = jnp.broadcast_to(m, (tok, HD))
        acc_ref[h] = o[:, :HD]
        l_ref[h] = o[:, HD:]


def far_kernel(last, tiers, n_refs, *refs):
    q_ref, rows_ref = refs[:2]
    piece_refs = refs[2 : 2 + n_refs]
    carry_in = refs[2 + n_refs : 5 + n_refs]
    m_in, l_in, acc_in = carry_in
    if last:
        out_hbm, s_ref, mx_ref, result, sems = refs[5 + n_refs :]
    else:
        *outs, s_ref, mx_ref = refs[5 + n_refs :]
    tok = q_ref.shape[0]
    heads = q_ref.shape[1] // HD
    first = rows_ref[0:1, 0:1]

    def leave(h):
        columns = slice(h * HD, (h + 1) * HD)
        return pltpu.make_async_copy(result.at[:, columns], out_hbm.at[:, columns], sems.at[h])

    def attend(pieces, bias):
        row_off = jnp.where(rows_ref[...] == first, 0.0, FAR)

        def score(h, slot):
            q = q_ref[:, h * HD : (h + 1) * HD]
            mx = None
            for k, (r, i) in enumerate(pieces):
                s = lax.dot_general(q, r[i + (slice(0, tok),)], NT, preferred_element_type=F32) + bias[k]
                s_ref[slot, :, k * tok : (k + 1) * tok] = s
                for t in range(tok // HD):
                    part = s[:, t * HD : (t + 1) * HD]
                    mx = part if mx is None else jnp.maximum(mx, part)
            mx_ref[slot] = mx

        def finish(h, slot):
            m_old = m_in[h]
            m_new = jnp.maximum(m_old, jnp.max(mx_ref[slot], 1, keepdims=True) - row_off)
            alpha = jnp.exp2((m_old - m_new) * FACTOR)
            shift = jnp.concatenate([m_new + row_off] * (tok // HD), 1) * FACTOR
            o = None
            for k, (r, i) in enumerate(pieces):
                s = s_ref[slot, :, k * tok : (k + 1) * tok]
                p = jnp.exp2(s * FACTOR - shift).astype(BF16)
                v = jnp.concatenate([r[i + (slice(tok, 2 * tok),)], jnp.ones((tok, HD), BF16)], 1)
                d = jnp.dot(p, v, preferred_element_type=F32)
                o = d if o is None else o + d
            acc = acc_in[h] * alpha + o[:, :HD]
            total = l_in[h] * alpha + o[:, HD:]
            if last:
                result[:, h * HD : (h + 1) * HD] = (acc / total).astype(BF16)
                leave(h).start()
            else:
                outs[0][h] = m_new
                outs[1][h] = total
                outs[2][h] = acc

        score(0, 0)
        for h in range(heads):
            if h + 1 < heads:
                score(h + 1, (h + 1) % 2)
            finish(h, h % 2)

    pieces, bias, seen = [], [], []
    for tier in tiers:
        new = [(piece_refs[n], i) for n, i in tier]
        pieces.append((pieces[-1] if pieces else []) + new)
        new_bias = [jnp.where(key_docs(r, i, tok) == first, 0.0, -FAR) for r, i in new]
        bias.append((bias[-1] if bias else []) + new_bias)
        seen.append(jnp.max(functools.reduce(jnp.maximum, new_bias)) == 0.0)

    farther = jnp.bool_(False)
    for t in reversed(range(len(tiers))):

        @pl.when(seen[t] & jnp.logical_not(farther))
        def _():
            attend(pieces[t], bias[t])

        farther = farther | seen[t]

    @pl.when(jnp.logical_not(farther))
    def _():
        for h in range(heads):
            if last:
                result[:, h * HD : (h + 1) * HD] = (acc_in[h] / l_in[h]).astype(BF16)
                leave(h).start()
            else:
                for ref, out in zip(carry_in, outs):
                    out[h] = ref[h]

    if last:
        for h in range(heads):
            leave(h).wait()


def lay_kernel(count, *refs):
    levels, outs = refs[: count + 1], refs[count + 1 :]
    y = lax.axis_index("ctx") % YS
    for by, out in enumerate(outs, 1):
        for k in range(count):

            @pl.when(y + by < YS)
            def _():
                out[k] = levels[k][...]

            @pl.when(y + by >= YS)
            def _():
                out[k] = levels[k + 1][...]


VM = pl.BlockSpec(memory_space=pltpu.VMEM)
HBM = pl.BlockSpec(memory_space=pltpu.HBM)


def params(mib=24):
    return pltpu.CompilerParams(vmem_limit_bytes=mib * 2**20)


def pack(kv, docs):
    tok = kv.shape[1]
    return pl.pallas_call(
        pack_kernel,
        grid=(1,),
        in_specs=[pl.BlockSpec(kv.shape, lambda i: (0, 0, 0)), pl.BlockSpec(docs.shape, lambda i: (0, 0))],
        out_specs=[VM, VM],
        out_shape=[jax.ShapeDtypeStruct((2 * tok + 16, HD), BF16), jax.ShapeDtypeStruct((tok, HD), F32)],
        compiler_params=params(),
        name="pack",
    )(kv, docs)


def carry_shapes(q):
    heads, tok = q.shape[1] // HD, q.shape[0]
    return [jax.ShapeDtypeStruct((heads, tok, HD), F32)] * 3


def cost(rows, keys):
    return pl.CostEstimate(flops=4 * rows * keys * HD, bytes_accessed=4 * rows * HD, transcendentals=rows * keys)


def own(q, rows, piece):
    return pl.pallas_call(
        own_kernel,
        in_specs=[VM] * 3,
        out_specs=[VM] * 3,
        out_shape=carry_shapes(q),
        compiler_params=params(),
        cost_estimate=cost(q.size // HD, q.shape[0]),
        name="own",
    )(q, rows, piece)


def far(q, rows, pieces, tiers, carry, last):
    tok = q.shape[0]
    n = sum(map(len, tiers))
    return pl.pallas_call(
        functools.partial(far_kernel, last, tiers, len(pieces)),
        in_specs=[VM] * (5 + len(pieces)),
        out_specs=HBM if last else [VM] * 3,
        out_shape=jax.ShapeDtypeStruct(q.shape, BF16) if last else carry_shapes(q),
        scratch_shapes=[pltpu.VMEM((2, tok, n * tok), F32), pltpu.VMEM((2, tok, HD), F32)]
        + [pltpu.VMEM(q.shape, BF16), pltpu.SemaphoreType.DMA((q.shape[1] // HD,))] * last,
        compiler_params=params(),
        cost_estimate=cost(q.size // HD, n * tok),
        name="far",
    )(q, rows, *pieces, *carry)


def lay(levels):
    count = len(levels) - 1
    return pl.pallas_call(
        functools.partial(lay_kernel, count),
        in_specs=[VM] * len(levels),
        out_specs=[VM] * (YS - 1),
        out_shape=[jax.ShapeDtypeStruct((count, *levels[0].shape), BF16)] * (YS - 1),
        compiler_params=params(),
        name="lay",
    )(*levels)


def on_device(queries, keys_values, segments):
    size = lax.axis_size("ctx")

    def up(x, by):
        return lax.ppermute(x, "ctx", [(c, c + by * YS) for c in range(size - by * YS)])

    def across(x, by):
        return lax.ppermute(x, "ctx", [(c, c - c % YS + (c + by) % YS) for c in range(size)])

    piece, rows = pack(keys_values, segments.reshape(-1, HD))
    two = up(piece, 2)
    one = up(piece, 1)
    carry = own(queries, rows, piece)
    two, carry = lax.optimization_barrier((two, carry))
    both = up(jnp.stack([one, two]), 2)
    near = [across(x, by) for by, x in enumerate(lay([piece, one, two]), 1)]
    carry = far(queries, rows, [one, two], [[(0, ()), (1, ())]], carry, False)
    both, carry = lax.optimization_barrier((both, carry))
    away = [across(x, by) for by, x in enumerate(lay([two, both[0], both[1]]), 1)]
    carry = far(
        queries,
        rows,
        [near[1], near[0], near[2], both],
        [[(0, (0,)), (1, (0,)), (2, (0,))], [(0, (1,)), (1, (1,)), (2, (1,)), (3, (0,))]],
        carry,
        False,
    )
    carry = far(queries, rows, [away[1], both], [[(0, (0,)), (0, (1,)), (1, (1,))]], carry, False)
    ends = [[(0, (0,)), (1, (0,)), (0, (1,)), (1, (1,))]]
    return far(queries, rows, [away[0], away[2]], ends, carry, True)


def solution(mesh):
    return jax.shard_map(
        on_device,
        mesh=mesh,
        in_specs=(P("ctx", "tp"), P(None, "ctx", "tp"), P("ctx")),
        out_specs=P("ctx", "tp"),
        check_vma=False,
    )
```
